256 devices in a mesh: dp: 4 (over y), pipe: 4 (over x), tensor: 16 (over z, core).
Axes of the slice: x: 4, y: 4, z: 8, core: 2. Of those that a mesh axis runs over, the one named last changes fastest.
Arguments:
- tokens: bfloat16 [2048, 3072], P(('dp', 'tensor')), may hold values from -6 to 6
- destination: int32 [2048], P(('dp', 'tensor')), may hold values from 0 to 2047, as said below
- segments: int32 [16, 128], P('dp'), may hold values from 0 to 5, never falling along the last dimension, each value on 1 to 64 neighbouring positions
- query_weight: bfloat16 [4, 3072, 2048], P('pipe', None, 'tensor')
- key_value_weight: bfloat16 [4, 3072, 2048], P('pipe', None, 'tensor')
- out_weight: bfloat16 [4, 2048, 3072], P('pipe', 'tensor'), may hold values from -0.125 to 0.125
- gate_weight: bfloat16 [4, 3072, 8192], P('pipe', None, 'tensor'), may hold values from -0.109375 to 0.109375
- up_weight: bfloat16 [4, 3072, 8192], P('pipe', None, 'tensor'), may hold values from -0.109375 to 0.109375
- down_weight: bfloat16 [4, 8192, 3072], P('pipe', 'tensor'), may hold values from -0.0625 to 0.0625
- attention_gain: float32 [4, 3072], P('pipe'), may hold values from 0.1 to 1.9
- forward_gain: float32 [4, 3072], P('pipe'), may hold values from 0.1 to 1.9
Outputs:
- layers_out: float32 [2048, 3072], P(('dp', 'pipe', 'tensor'))
The draws below stay inside these ranges and needn't reach their ends.
Inputs may be any that keep to these rules, and one draw needn't show every extreme that they name: destination is a permutation of the 2048 rows. A row held at tensor index t goes to a place within its micro-batch in [t * 8, (t + 1) * 8). At most 16 rows of one device go to one dp index, and every device sends exactly 16 rows to some dp index.
All inputs are finite; a program needn't handle non-finite values.
Results may differ from the reference program's by a relative error of at most 0.04.
Values may be sent and summed in bfloat16 or wider, within the bound.
No kernel may reach another device: no remote copies, remote signals or barrier semaphores. Data moves between devices by JAX's collectives and lax.ppermute only.
A program may use at most 64 MiB of HBM per device.

```python
import math
import jax
import jax.numpy as jnp
import numpy as np
from jax import lax

D = 3072
H = 16
KV = 8
HD = 128
FF = 8192
MB = 128
DOCS = 6
MICRO = 4
LAYERS = 4
TOKENS = 2048
ROWS = 32
CAP = 16
N_DP = 4
N_TENSOR = 16


def shared_keys(key):
    return jax.random.normal(key, (LAYERS, D, KV, 2, HD), jnp.float32) * D ** (-0.5)


def draw_key_value_weight(key, part):
    base = shared_keys(key)
    return base.reshape(LAYERS, D, 2 * KV * HD).astype(jnp.bfloat16)


def draw_query_weight(key, part):
    key = jax.random.fold_in(key, 7)
    own = jax.random.normal(key, (LAYERS, D, H, HD), jnp.float32) * D ** (-0.5)
    return own.reshape(LAYERS, D, H * HD).astype(jnp.bfloat16)


def draw_destination(key, part):
    key = jax.random.fold_in(key, 5)
    slab_rows = MB // N_TENSOR

    def one_slot(slot_key, tensor_index):
        cut_key, top_key, place_key, order_key = jax.random.split(slot_key, 4)
        cuts = jnp.sort(jax.random.randint(cut_key, (N_DP - 2,), 0, ROWS - CAP + 1))
        edges = jnp.concatenate([jnp.zeros((1,), jnp.int32), cuts.astype(jnp.int32), jnp.full((1,), ROWS - CAP, jnp.int32)])
        others = edges[1:] - edges[:-1]
        amounts = jnp.roll(jnp.concatenate([jnp.full((1,), CAP, jnp.int32), others]), jax.random.randint(top_key, (), 0, N_DP))
        ends = jnp.cumsum(amounts)
        order = jnp.arange(ROWS, dtype=jnp.int32)
        offset = jnp.sum((order[:, None] >= ends[None, :]).astype(jnp.int32), axis=1)
        places = jnp.stack([jax.random.permutation(jax.random.fold_in(place_key, group), ROWS) for group in range(N_DP)]).astype(jnp.int32)
        orders = jnp.stack([jax.random.permutation(jax.random.fold_in(order_key, group), ROWS) for group in range(N_DP)]).astype(jnp.int32)
        groups = jnp.arange(N_DP, dtype=jnp.int32)
        target = (groups[:, None] + offset[None, :]) % N_DP
        landing = places[target, order[None, :]]
        value = target * (MICRO * MB) + landing // slab_rows * MB + tensor_index * slab_rows + landing % slab_rows
        return jnp.zeros((N_DP, ROWS), jnp.int32).at[jnp.broadcast_to(groups[:, None], (N_DP, ROWS)), orders].set(value)
    table = jax.vmap(one_slot)(jax.random.split(key, N_TENSOR), jnp.arange(N_TENSOR, dtype=jnp.int32))
    return jnp.transpose(table, (1, 0, 2)).reshape(TOKENS)


def block_scale(key, dims, cuts, least, top_value):
    factor_of, own = 1.0, jax.random.fold_in(key, 6)
    for dim, blocks in cuts:
        heights = jnp.exp(jax.random.uniform(jax.random.fold_in(own, dim), (blocks,), jnp.float32, least / len(cuts), top_value / len(cuts)))
        factor_of = factor_of * jnp.repeat(heights, dims[dim] // blocks).reshape([-1 if axis == dim else 1 for axis in range(len(dims))])
    return factor_of


def split_up(count, total, most, lean):
    portions = [(1 << 20) // math.isqrt(standing ** lean) + 1 for standing in range(2, count + 1)]
    surplus, given = total - most - (count - 1), [1] * (count - 1)
    while surplus > 0:
        free = [i for i in range(count - 1) if given[i] < most]
        mass, budget = sum([portions[i] for i in free]), surplus
        for i in free:
            more = min(most - given[i], max(1, budget * portions[i] // mass), surplus)
            given[i] = given[i] + more
            surplus = surplus - more
    return np.array([most] + given)


def ragged_sizes(own_key, amount, total, most, skew):
    if amount == 2:
        one = jax.random.randint(own_key, (), max(1, total - most), min(most, total - 1) + 1)
        return jnp.stack([one, total - one])
    tallies = jnp.asarray(split_up(amount, total, most, skew), jnp.int32)
    twos = (amount - 1) // 2
    giver, receiver = tallies[1:1 + 2 * twos:2], tallies[2:2 + 2 * twos:2]
    room = jnp.minimum(giver - 1, most - receiver)
    shifted = jax.random.randint(jax.random.fold_in(own_key, 1), (twos,), 0, 1 << 20) % (room + 1)
    tallies = tallies.at[1:1 + 2 * twos:2].set(giver - shifted).at[2:2 + 2 * twos:2].set(receiver + shifted)
    return tallies[jax.random.permutation(jax.random.fold_in(own_key, 2), amount)]


def normal_values(stream_key, shape, deviation, most, pieces=(), kind=jnp.bfloat16):
    array = jax.random.normal(stream_key, shape, jnp.float32) * deviation
    if len(pieces) > 0:
        array = block_scale(stream_key, shape, pieces, -0.22, 0.18) * array
    return jnp.clip(array, min=-most, max=most).astype(kind)


def setup_inputs(seed: int = 0) -> dict:
    seeds = jax.random.split(jax.random.key(seed), 12)
    tokens = normal_values(seeds[0], (TOKENS, D), 1.0, 6.0, ((0, 64),))
    destination = draw_destination(jax.random.fold_in(seeds[11], 71), 0)
    segments = jax.vmap(lambda own: jnp.searchsorted(jnp.cumsum(ragged_sizes(own, DOCS, MB, MB // 2, 2)), jnp.arange(MB), side="right"))(jax.random.split(seeds[2], (N_DP * MICRO))).reshape((N_DP * MICRO, MB)).astype(jnp.int32)
    query_weight = draw_query_weight(jax.random.fold_in(seeds[11], 71), 0)
    key_value_weight = draw_key_value_weight(jax.random.fold_in(seeds[11], 71), 0)
    out_weight = normal_values(seeds[5], (LAYERS, H * HD, D), (H * HD) ** -0.5, 0.125, ((0, 4), (1, 16)))
    gate_weight = normal_values(seeds[6], (LAYERS, D, FF), D ** -0.5, 0.109375, ((0, 4), (2, 16)))
    up_weight = normal_values(seeds[7], (LAYERS, D, FF), D ** -0.5, 0.109375, ((0, 4), (2, 16)))
    down_weight = normal_values(seeds[8], (LAYERS, FF, D), FF ** -0.5, 0.0625, ((0, 4), (1, 16)))
    attention_gain = jnp.clip(1.0 + 0.18 * jax.random.normal(seeds[9], (LAYERS, D), jnp.float32), 0.1, 1.9)
    forward_gain = jnp.clip(1.0 + 0.18 * jax.random.normal(seeds[10], (LAYERS, D), jnp.float32), 0.1, 1.9)
    return {"tokens": tokens, "destination": destination, "segments": segments, "query_weight": query_weight, "key_value_weight": key_value_weight, "out_weight": out_weight, "gate_weight": gate_weight, "up_weight": up_weight, "down_weight": down_weight, "attention_gain": attention_gain, "forward_gain": forward_gain}


def doc_positions(doc_ids):
    order = jnp.arange(doc_ids.shape[0], dtype=jnp.int32)
    change = jnp.concatenate([jnp.ones((1,), dtype=bool), doc_ids[1:] != doc_ids[:-1]])
    starts = lax.cummax(jnp.where(change, order, jnp.zeros_like(order)), axis=0)
    return (order - starts).astype(jnp.float32)

def rotate(stack, places):
    half_width = stack.shape[-1] // 2
    frequency = 500000.0 ** (-(jnp.arange(half_width, dtype=jnp.float32) * 2.0 / stack.shape[-1]))
    angles = places[:, None] * frequency[None, :]
    cosine = jnp.cos(angles)[:, None, :]
    sine_part = jnp.sin(angles)[:, None, :]
    front_half = stack[..., :half_width]
    back_half = stack[..., half_width:]
    return jnp.concatenate([front_half * cosine - back_half * sine_part, back_half * cosine + front_half * sine_part], axis=-1)

def normalize(rows_in, gain):
    values = rows_in.astype(jnp.float32)
    meansq = lax.optimization_barrier(jnp.mean(values * values, axis=-1, keepdims=True))
    return (values * lax.rsqrt(meansq + 1e-05) * gain.astype(jnp.float32)).astype(jnp.bfloat16)

def visible(doc_ids):
    order = jnp.arange(doc_ids.shape[0], dtype=jnp.int32)
    return jnp.logical_and(doc_ids[:, None] == doc_ids[None, :], order[None, :] <= order[:, None])

def attend(queries, key_heads, value_heads, doc_ids):
    rows, heads_here, head_width = queries.shape
    shared_heads = key_heads.shape[1]
    grouped_queries = queries.reshape(rows, shared_heads, heads_here // shared_heads, head_width).astype(jnp.float32)
    scores = jnp.einsum('qagd,kad->agqk', grouped_queries, key_heads.astype(jnp.float32), precision=lax.Precision.HIGHEST) * head_width ** (-0.5)
    scores = jnp.where(visible(doc_ids), scores, jnp.float32(-1e+30))
    row_max = lax.optimization_barrier(jnp.max(scores, axis=-1, keepdims=True))
    spread = jnp.exp(scores - row_max)
    weights = (spread / lax.optimization_barrier(jnp.sum(spread, axis=-1, keepdims=True))).astype(jnp.bfloat16)
    mixed = jnp.einsum('agqk,kad->qagd', weights.astype(jnp.float32), value_heads.astype(jnp.float32))
    return mixed.astype(jnp.bfloat16).reshape(rows, heads_here * head_width)

def grouped_sum(left, right, group_count):
    rows, inner = left.shape
    left_groups = left.reshape(rows, group_count, inner // group_count).astype(jnp.float32)
    right_groups = right.reshape(group_count, inner // group_count, right.shape[1]).astype(jnp.float32)
    parts = jnp.einsum('rgk,gkd->grd', left_groups, right_groups)
    rounded = lax.optimization_barrier(parts.astype(jnp.bfloat16))
    return lax.optimization_barrier(jnp.sum(rounded.astype(jnp.float32), axis=0))

def layer_step(rows_now, doc_ids, query_local, pair_local, out_local, gate_local, up_local, down_local, gain_attention, gain_forward):
    places = doc_positions(doc_ids)
    normed = normalize(rows_now, gain_attention)
    query_proj = jnp.dot(normed, query_local, preferred_element_type=jnp.float32)
    queries = rotate(query_proj.reshape(MB, H, HD), places)
    pairs = jnp.dot(normed, pair_local, preferred_element_type=jnp.float32).reshape(MB, KV, 2, HD)
    key_heads = rotate(pairs[:, :, 0], places)
    value_heads = pairs[:, :, 1].astype(jnp.bfloat16)
    mixed = attend(queries, key_heads, value_heads, doc_ids)
    attn_total = grouped_sum(mixed, out_local, N_TENSOR)
    halfway = rows_now + attn_total
    normed_two = normalize(halfway, gain_forward)
    gate = jnp.dot(normed_two, gate_local, preferred_element_type=jnp.float32)
    upward = jnp.dot(normed_two, up_local, preferred_element_type=jnp.float32)
    hidden = (jax.nn.silu(gate) * upward).astype(jnp.bfloat16)
    forward_total = grouped_sum(hidden, down_local, N_TENSOR)
    return halfway + forward_total

def reference(tokens, destination, segments, query_weight, key_value_weight, out_weight, gate_weight, up_weight, down_weight, attention_gain, forward_gain):
    regrouped = jnp.zeros_like(tokens).at[destination].set(tokens)
    batches = regrouped.reshape(N_DP * MICRO, MB, D)

    def run(item):
        rows_in, doc_ids = item
        rows_now = rows_in.astype(jnp.float32)
        for layer in range(LAYERS):
            rows_now = layer_step(rows_now, doc_ids, query_weight[layer], key_value_weight[layer], out_weight[layer], gate_weight[layer], up_weight[layer], down_weight[layer], attention_gain[layer], forward_gain[layer])
        return rows_now
    return lax.map(run, (batches, segments)).reshape(TOKENS, D)
```

```python
import jax
import jax.numpy as jnp
from jax import lax
from jax.sharding import PartitionSpec as P

HD = 128


def swapped(value, axis, apart):
    mask = 2**apart
    pairs = [(source, source ^ mask) for source in range(lax.axis_size(axis))]
    return lax.ppermute(value, axis, pairs)


def same_core_groups():
    peers = lax.axis_size("tensor")
    return [list(range(core, peers, 2)) for core in range(2)]


def scatter_sum(left, weight):
    chips = lax.axis_size("tensor") // 2
    rows = left.shape[0] // (2 * chips)
    parity = lax.axis_index("tensor") % 2
    split = left.reshape(chips, 2, rows, -1)
    mine = jnp.where(parity == 0, split[:, 0], split[:, 1])
    other = jnp.where(parity == 0, split[:, 1], split[:, 0])
    ordered = jnp.concatenate([other, mine], axis=0).reshape(left.shape)
    part = jnp.dot(ordered, weight, preferred_element_type=jnp.float32)
    half = chips * rows
    got = swapped(part[:half].astype(jnp.bfloat16), "tensor", 0)
    pair = (part[half:] + got.astype(jnp.float32)).astype(jnp.bfloat16)
    blocks = lax.all_to_all(
        pair.reshape(chips, rows, -1),
        "tensor",
        split_axis=0,
        concat_axis=0,
        tiled=True,
        axis_index_groups=same_core_groups(),
    )
    return jnp.sum(blocks.astype(jnp.float32), axis=0)


def doc_positions(doc_ids):
    order = jnp.arange(doc_ids.shape[0], dtype=jnp.int32)
    change = jnp.concatenate([jnp.ones((1,), dtype=bool), doc_ids[1:] != doc_ids[:-1]])
    starts = lax.cummax(jnp.where(change, order, jnp.zeros_like(order)), axis=0)
    return (order - starts).astype(jnp.float32)


def rotate(stack, places):
    half_width = stack.shape[-1] // 2
    frequency = 500000.0 ** (-(jnp.arange(half_width, dtype=jnp.float32) * 2.0 / stack.shape[-1]))
    angles = places[:, None] * frequency[None, :]
    cosine = jnp.cos(angles)[:, None, :]
    sine_part = jnp.sin(angles)[:, None, :]
    front_half = stack[..., :half_width]
    back_half = stack[..., half_width:]
    return jnp.concatenate(
        [front_half * cosine - back_half * sine_part, back_half * cosine + front_half * sine_part],
        axis=-1,
    )


def normalize(rows_in, gain):
    meansq = jnp.mean(rows_in * rows_in, axis=-1, keepdims=True)
    return (rows_in * lax.rsqrt(meansq + 1e-05) * gain).astype(jnp.bfloat16)


def visible(doc_ids):
    order = jnp.arange(doc_ids.shape[0], dtype=jnp.int32)
    return jnp.logical_and(doc_ids[:, None] == doc_ids[None, :], order[None, :] <= order[:, None])


def attend(queries, key_heads, value_heads, doc_ids):
    rows, heads_here, head_width = queries.shape
    shared_heads = key_heads.shape[1]
    grouped_queries = queries.reshape(rows, shared_heads, heads_here // shared_heads, head_width)
    scores = jnp.einsum(
        "qagd,kad->agqk",
        grouped_queries,
        key_heads,
        precision=lax.Precision.HIGHEST,
        preferred_element_type=jnp.float32,
    ) * head_width ** (-0.5)
    scores = jnp.where(visible(doc_ids), scores, jnp.float32(-1e30))
    row_max = jnp.max(scores, axis=-1, keepdims=True)
    spread = jnp.exp(scores - row_max)
    weights = (spread / jnp.sum(spread, axis=-1, keepdims=True)).astype(jnp.bfloat16)
    mixed = jnp.einsum("agqk,kad->qagd", weights, value_heads, preferred_element_type=jnp.float32)
    return mixed.astype(jnp.bfloat16).reshape(rows, heads_here * head_width)


def expand(rows_in, gate_local, up_local):
    gate = jnp.dot(rows_in, gate_local, preferred_element_type=jnp.float32)
    upward = jnp.dot(rows_in, up_local, preferred_element_type=jnp.float32)
    return (jax.nn.silu(gate) * upward).astype(jnp.bfloat16)


def split_pairs(pairs, places):
    rows = pairs.shape[0]
    parity = lax.axis_index("tensor") % 2
    turned = rotate(pairs.reshape(rows, 1, HD), places).reshape(rows, HD)
    mine = jnp.where(parity == 0, turned, pairs)
    partner = swapped(mine.astype(jnp.bfloat16), "tensor", 0).astype(mine.dtype)
    key_heads = jnp.where(parity == 0, mine, partner).reshape(rows, 1, HD)
    value_heads = jnp.where(parity == 0, partner, mine).astype(jnp.bfloat16).reshape(rows, 1, HD)
    return (key_heads, value_heads)


def run_layer(current, doc_ids, layer_weights):
    (
        query_local,
        pair_local,
        out_local,
        gate_local,
        up_local,
        down_local,
        gain_attention,
        gain_forward,
    ) = layer_weights
    micro_rows = doc_ids.shape[0]
    query_cols = query_local.shape[1]
    places = doc_positions(doc_ids)
    piece = lax.all_gather(normalize(current, gain_attention), "tensor", axis=0, tiled=True)
    projected = jnp.concatenate(
        [
            jnp.dot(piece, query_local, preferred_element_type=jnp.float32),
            jnp.dot(piece, pair_local, preferred_element_type=jnp.float32),
        ],
        axis=1,
    )
    heads_here = query_cols // HD
    queries = rotate(projected[:, :query_cols].reshape(micro_rows, heads_here, HD), places)
    key_heads, value_heads = split_pairs(projected[:, query_cols:], places)
    mixed = attend(queries, key_heads, value_heads, doc_ids)
    total = scatter_sum(mixed, out_local)
    halfway = current + total
    hidden = expand(
        lax.all_gather(normalize(halfway, gain_forward), "tensor", axis=0, tiled=True),
        gate_local,
        up_local,
    )
    forward = scatter_sum(hidden, down_local)
    return halfway + forward


def pass_on(result, moment, micro_count):
    last = lax.axis_size("pipe") - 1
    pairs = [(i, i + 1) for i in range(last) if 0 <= moment - i < micro_count]
    if moment >= last:
        pairs.append((last, moment - last))
    return lax.ppermute(result.astype(jnp.bfloat16), "pipe", pairs).astype(jnp.float32)


def shards(
    tokens,
    destination,
    segments,
    query_weight,
    key_value_weight,
    out_weight,
    gate_weight,
    up_weight,
    down_weight,
    attention_gain,
    forward_gain,
):
    group_count = lax.axis_size("dp")
    tensor_count = lax.axis_size("tensor")
    pipe_count = lax.axis_size("pipe")
    micro_count, micro_rows = segments.shape
    slab_rows = micro_rows // tensor_count
    held_rows, width = tokens.shape
    capacity = held_rows // 2
    group_span = micro_count * micro_rows
    target = destination // group_span
    within = destination % group_span
    landing = within // micro_rows * slab_rows + within % slab_rows
    member = (target[:, None] == jnp.arange(group_count, dtype=jnp.int32)[None, :]).astype(
        jnp.int32
    )
    before = jnp.sum((jnp.cumsum(member, axis=0) - member) * member, axis=1)
    slot_index = target * capacity + before
    send_rows = jnp.zeros((group_count * capacity, width), jnp.bfloat16).at[slot_index].set(tokens)
    send_places = (
        jnp.full((group_count * capacity,), held_rows, jnp.int32).at[slot_index].set(landing)
    )
    got_rows, got_places = (
        lax.all_to_all(
            send_rows.reshape(group_count, capacity, width),
            "dp",
            split_axis=0,
            concat_axis=0,
            tiled=True,
        ),
        lax.all_to_all(
            send_places.reshape(group_count, capacity),
            "dp",
            split_axis=0,
            concat_axis=0,
            tiled=True,
        ),
    )
    regrouped = (
        jnp.zeros((held_rows, width), jnp.bfloat16)
        .at[got_places.reshape(-1)]
        .set(got_rows.reshape(-1, width), mode="drop")
    )
    micro_batches = regrouped.reshape(micro_count, slab_rows, width)
    layer_weights = (
        query_weight[0],
        key_value_weight[0],
        out_weight[0],
        gate_weight[0],
        up_weight[0],
        down_weight[0],
        attention_gain[0],
        forward_gain[0],
    )
    phase_index = lax.axis_index("pipe")
    carried = jnp.zeros((slab_rows, width), jnp.float32)
    out = jnp.zeros((slab_rows, width), jnp.float32)
    for moment in range(micro_count + pipe_count - 1):
        feed_rows = micro_batches[min(moment, micro_count - 1)].astype(jnp.float32)
        current = jnp.where(
            jnp.logical_and(phase_index == 0, moment < micro_count), feed_rows, carried
        )
        micro_index = jnp.clip(moment - phase_index, 0, micro_count - 1)
        doc_ids = lax.dynamic_index_in_dim(segments, micro_index, 0, keepdims=False)
        result = run_layer(current, doc_ids, layer_weights)
        home = moment - (pipe_count - 1)
        if moment < micro_count + pipe_count - 2:
            carried = pass_on(result, moment, micro_count)
            if home >= 0:
                out = jnp.where(phase_index == home, carried, out)
        else:
            out = jnp.where(phase_index == home, result, out)
    return out


def solution(mesh):
    placed = (
        P(("dp", "tensor"), None),
        P(("dp", "tensor")),
        P("dp", None),
        P("pipe", None, "tensor"),
        P("pipe", None, "tensor"),
        P("pipe", "tensor", None),
        P("pipe", None, "tensor"),
        P("pipe", None, "tensor"),
        P("pipe", "tensor", None),
        P("pipe", None),
        P("pipe", None),
    )
    return jax.shard_map(
        shards,
        mesh=mesh,
        in_specs=placed,
        out_specs=P(("dp", "pipe", "tensor"), None),
        check_vma=False,
    )
```

```python
import jax
import jax.numpy as jnp
from jax import lax
from jax.experimental import pallas as pl
from jax.experimental.pallas import tpu as pltpu
from jax.sharding import PartitionSpec as P

HD = 128
CORES = 2
VMEM_LIMIT = 52 * 2**20


def swapped(value):
    pairs = [(source, source ^ 1) for source in range(lax.axis_size("tensor"))]
    return lax.ppermute(value, "tensor", pairs)


def parity():
    return lax.axis_index("tensor") % CORES


def scatter_sum(left, weight):
    peers = lax.axis_size("tensor")
    chips = peers // CORES
    rows = left.shape[0] // peers
    split = left.reshape(chips, CORES, rows, -1)
    mine = jnp.where(parity() == 0, split[:, 0], split[:, 1])
    other = jnp.where(parity() == 0, split[:, 1], split[:, 0])
    ordered = jnp.concatenate([other, mine], axis=0).reshape(left.shape)
    part = jnp.dot(ordered, weight, preferred_element_type=jnp.float32)
    half = chips * rows
    got = swapped(part[:half].astype(jnp.bfloat16))
    pair = (part[half:] + got.astype(jnp.float32)).astype(jnp.bfloat16)
    blocks = lax.all_to_all(
        pair.reshape(chips, rows, -1),
        "tensor",
        split_axis=0,
        concat_axis=0,
        tiled=True,
        axis_index_groups=[list(range(core, peers, CORES)) for core in range(CORES)],
    )
    return jnp.sum(blocks.astype(jnp.float32), axis=0)


def tables(doc_ids):
    order = jnp.arange(doc_ids.shape[1], dtype=jnp.int32)
    same = doc_ids[:, :, None] == doc_ids[:, None, :]
    seen = jnp.logical_and(same, order[None, :] <= order[:, None])
    places = jnp.sum(seen.astype(jnp.float32), axis=-1) - 1.0
    half = HD // 2
    frequency = 500000.0 ** (-(jnp.arange(half, dtype=jnp.float32) * 2.0 / HD))
    angles = places[:, :, None] * frequency
    cosine, sine = jnp.cos(angles), jnp.sin(angles)
    return (
        jnp.concatenate([cosine, cosine], axis=-1),
        jnp.concatenate([-sine, sine], axis=-1),
        seen.astype(jnp.float32),
    )


def normalize(rows_in, gain):
    meansq = jnp.mean(rows_in * rows_in, axis=-1, keepdims=True)
    return (rows_in * lax.rsqrt(meansq + 1e-05) * gain).astype(jnp.bfloat16)


def split_float(values):
    high = values.astype(jnp.bfloat16)
    return high, (values - high.astype(jnp.float32)).astype(jnp.bfloat16)


def attend(queries, keys, values, seen):
    query_high, query_low = split_float(queries)
    key_high, key_low = split_float(keys)
    scores = lax.dot_general(
        jnp.concatenate([query_high, query_high, query_low], axis=1),
        jnp.concatenate([key_high, key_low, key_high], axis=1),
        (((1,), (1,)), ((), ())),
        preferred_element_type=jnp.float32,
    ) * HD ** (-0.5)
    scores = jnp.where(seen > 0.5, scores, jnp.float32(-1e30))
    spread = jnp.exp(scores - jnp.max(scores, axis=-1, keepdims=True))
    weights = (spread / jnp.sum(spread, axis=-1, keepdims=True)).astype(jnp.bfloat16)
    return jnp.dot(weights, values, preferred_element_type=jnp.float32).astype(jnp.bfloat16)


def attend_local(piece, query_local, pair_local, turns):
    cosine, sine, seen = turns

    def turn(head):
        front, back = head[:, : HD // 2], head[:, HD // 2 :]
        return head * cosine + jnp.concatenate([back, front], axis=1) * sine

    queries = turn(jnp.dot(piece, query_local, preferred_element_type=jnp.float32))
    pair = jnp.dot(piece, pair_local, preferred_element_type=jnp.float32)
    mine = jnp.where(parity() == 0, turn(pair), pair)
    partner = swapped(mine.astype(jnp.bfloat16)).astype(mine.dtype)
    keys = jnp.where(parity() == 0, mine, partner)
    values = jnp.where(parity() == 0, partner, mine).astype(jnp.bfloat16)
    return attend(queries, keys, values, seen)


def whole_projections(query_local, pair_local):
    both = jnp.concatenate([query_local, pair_local], axis=1)
    half = both.shape[0] // 2
    first, second = both[:half], both[half:]
    kept = jnp.where(parity() == 0, first, second)
    got = swapped(jnp.where(parity() == 0, second, first))
    block = jnp.where(
        parity() == 0,
        jnp.concatenate([kept, got], axis=1),
        jnp.concatenate([got, kept], axis=1),
    )
    whole = lax.all_gather(block, "tensor", axis=0, tiled=True)
    return whole.reshape(-1, 2 * half, block.shape[1])


def attention_body(
    where_ref,
    x_ref,
    gain_ref,
    cosine_ref,
    sine_ref,
    seen_ref,
    in_hbm,
    out_hbm,
    total_ref,
    normed_ref,
    in_ref,
    out_ref,
    in_sem,
    out_sem,
):
    groups = in_ref.shape[0]
    rows, width = x_ref.shape
    inner = out_hbm.shape[2]
    strip = 16
    micro, core = where_ref[0], where_ref[1]
    fetch_in = [
        pltpu.make_async_copy(in_hbm.at[group, core], in_ref.at[group], in_sem.at[group])
        for group in range(groups)
    ]
    fetch_out = [
        pltpu.make_async_copy(
            out_hbm.at[group, core],
            out_ref.at[pl.ds(group * inner, inner), :],
            out_sem.at[group],
        )
        for group in range(groups)
    ]
    for copy in fetch_in + fetch_out:
        copy.start()

    @pl.loop(0, rows // strip)
    def _(index):
        part = pl.ds(pl.multiple_of(index * strip, strip), strip)
        normed_ref[part, :] = normalize(x_ref[part, :].astype(jnp.float32), gain_ref[...])

    cosine, sine, seen = cosine_ref[micro], sine_ref[micro], seen_ref[micro]
    seen_twice = jnp.concatenate([seen, seen], axis=0)

    def turn(head):
        return head * cosine + pltpu.roll(head, HD // 2, 1) * sine

    def project(group):
        fetch_in[group].wait()
        return jnp.dot(normed_ref[...], in_ref[group], preferred_element_type=jnp.float32)

    mixed = []
    heads = project(0)
    for group in range(groups):
        later = project(group + 1) if group + 1 < groups else None
        queries = jnp.concatenate(
            [turn(heads[:, :HD]), turn(heads[:, 2 * HD : 3 * HD])], axis=0
        )
        both = attend(
            queries,
            turn(heads[:, HD : 2 * HD]),
            heads[:, 3 * HD :].astype(jnp.bfloat16),
            seen_twice,
        )
        mixed += [both[:rows], both[rows:]]
        heads = later
    left = jnp.concatenate(mixed, axis=1)
    for copy in fetch_out:
        copy.wait()
    tile = 512

    @pl.loop(0, width // tile)
    def _(index):
        part = pl.ds(pl.multiple_of(index * tile, tile), tile)
        total_ref[:, part] = jnp.dot(
            left, out_ref[:, part], preferred_element_type=jnp.float32
        ).astype(jnp.bfloat16)


def attention_half(everyone, micro_index, turns, whole_in, whole_out, gain):
    rows, width = everyone.shape
    chips, _, columns = whole_in.shape
    groups = chips // CORES
    inner = whole_out.shape[0] // chips
    vmem = pl.BlockSpec(memory_space=pltpu.VMEM)
    hbm = pl.BlockSpec(memory_space=pltpu.HBM)
    return pl.pallas_call(
        attention_body,
        in_specs=[pl.BlockSpec(memory_space=pltpu.SMEM)] + [vmem] * 5 + [hbm] * 2,
        out_specs=vmem,
        scratch_shapes=[
            pltpu.VMEM((rows, width), jnp.bfloat16),
            pltpu.VMEM((groups, width, columns), jnp.bfloat16),
            pltpu.VMEM((groups * inner, width), jnp.bfloat16),
            pltpu.SemaphoreType.DMA((groups,)),
            pltpu.SemaphoreType.DMA((groups,)),
        ],
        out_shape=jax.ShapeDtypeStruct((rows, width), jnp.bfloat16),
        compiler_params=pltpu.CompilerParams(vmem_limit_bytes=VMEM_LIMIT),
        cost_estimate=pl.CostEstimate(
            flops=2 * rows * width * groups * (columns + inner),
            bytes_accessed=2 * width * groups * (columns + inner),
            transcendentals=2 * rows * rows * groups,
        ),
    )(
        jnp.stack([micro_index, parity()]).astype(jnp.int32),
        everyone,
        gain[None],
        *turns,
        whole_in.reshape(groups, CORES, width, columns),
        whole_out.reshape(groups, CORES, inner, width),
    )


def run_layer(current, micro_index, turns, layer_weights, whole_in, whole_out):
    (
        query_local,
        pair_local,
        out_local,
        gate_local,
        up_local,
        down_local,
        gain_attention,
        gain_forward,
    ) = layer_weights
    slab_rows = current.shape[0]
    everyone = lax.all_gather(current, "tensor", axis=0, tiled=True)
    if whole_in is not None:
        part = attention_half(everyone, micro_index, turns, whole_in, whole_out, gain_attention)
        total = part.astype(jnp.float32) + swapped(part).astype(jnp.float32)
    else:
        now = [lax.dynamic_index_in_dim(table, micro_index, 0, keepdims=False) for table in turns]
        piece = normalize(everyone.astype(jnp.float32), gain_attention)
        mixed = attend_local(piece, query_local, pair_local, now)
        if whole_out is not None:
            heads = lax.all_gather(mixed, "tensor", axis=1, tiled=True)
            total = jnp.dot(heads, whole_out, preferred_element_type=jnp.float32)
    if whole_out is not None:
        halfway_all = everyone.astype(jnp.float32) + total
        piece = normalize(halfway_all, gain_forward)
        start = lax.axis_index("tensor") * slab_rows
        halfway = lax.dynamic_slice_in_dim(halfway_all, start, slab_rows, 0)
    else:
        halfway = current.astype(jnp.float32) + scatter_sum(mixed, out_local)
        piece = lax.all_gather(normalize(halfway, gain_forward), "tensor", axis=0, tiled=True)
    gate = jnp.dot(piece, gate_local, preferred_element_type=jnp.float32)
    upward = jnp.dot(piece, up_local, preferred_element_type=jnp.float32)
    hidden = (jax.nn.silu(gate) * upward).astype(jnp.bfloat16)
    return halfway + scatter_sum(hidden, down_local)


def pass_on(result, moment, micro_count):
    last = lax.axis_size("pipe") - 1
    pairs = [(i, i + 1) for i in range(last) if 0 <= moment - i < micro_count]
    if moment >= last:
        pairs.append((last, moment - last))
    return lax.ppermute(result.astype(jnp.bfloat16), "pipe", pairs)


def regroup(tokens, destination, group_count, group_span, micro_rows, slab_rows):
    held_rows, width = tokens.shape
    capacity = held_rows // 2
    slots = group_count * capacity
    target = destination // group_span
    within = destination % group_span
    landing = within // micro_rows * slab_rows + within % slab_rows
    order = jnp.arange(held_rows, dtype=jnp.int32)
    ahead = jnp.logical_and(target[:, None] == target[None, :], order[None, :] < order[:, None])
    slot_index = target * capacity + jnp.sum(ahead.astype(jnp.int32), axis=1)
    to_slot = jnp.arange(slots, dtype=jnp.int32)[:, None] == slot_index[None, :]
    mark = jnp.broadcast_to((landing + 1).astype(jnp.bfloat16)[:, None], (held_rows, HD))
    sent = jnp.dot(
        to_slot.astype(jnp.bfloat16),
        jnp.concatenate([tokens, mark], axis=1),
        preferred_element_type=jnp.float32,
    ).astype(jnp.bfloat16)
    got = lax.all_to_all(
        sent.reshape(group_count, capacity, width + HD),
        "dp",
        split_axis=0,
        concat_axis=0,
        tiled=True,
    ).reshape(slots, width + HD)
    place = got[:, width].astype(jnp.int32) - 1
    to_row = order[:, None] == place[None, :]
    return jnp.dot(
        to_row.astype(jnp.bfloat16), got[:, :width], preferred_element_type=jnp.float32
    ).astype(jnp.bfloat16)


def shards(
    tokens,
    destination,
    segments,
    query_weight,
    key_value_weight,
    out_weight,
    gate_weight,
    up_weight,
    down_weight,
    attention_gain,
    forward_gain,
):
    pipe_count = lax.axis_size("pipe")
    micro_count, micro_rows = segments.shape
    slab_rows = micro_rows // lax.axis_size("tensor")
    width = tokens.shape[1]
    whole_out = lax.all_gather(out_weight[0], "tensor", axis=0, tiled=True)
    whole_in = whole_projections(query_weight[0], key_value_weight[0])
    regrouped = regroup(
        tokens,
        destination,
        lax.axis_size("dp"),
        micro_count * micro_rows,
        micro_rows,
        slab_rows,
    )
    micro_batches = regrouped.reshape(micro_count, slab_rows, width)
    turns = tables(segments)
    layer_weights = (
        query_weight[0],
        key_value_weight[0],
        out_weight[0],
        gate_weight[0],
        up_weight[0],
        down_weight[0],
        attention_gain[0],
        forward_gain[0],
    )
    phase_index = lax.axis_index("pipe")
    carried = jnp.zeros((slab_rows, width), jnp.bfloat16)
    out = jnp.zeros((slab_rows, width), jnp.float32)
    for moment in range(micro_count + pipe_count - 1):
        current = carried
        if moment < micro_count:
            current = jnp.where(phase_index == 0, micro_batches[moment], carried)
        micro_index = jnp.clip(moment - phase_index, 0, micro_count - 1)
        result = run_layer(
            current,
            micro_index,
            turns,
            layer_weights,
            None if moment < 2 else whole_in,
            None if moment < 1 else whole_out,
        )
        home = moment - (pipe_count - 1)
        if moment < micro_count + pipe_count - 2:
            carried = pass_on(result, moment, micro_count)
            if home >= 0:
                out = jnp.where(phase_index == home, carried.astype(jnp.float32), out)
        else:
            out = jnp.where(phase_index == home, result, out)
    return out


def solution(mesh):
    placed = (
        P(("dp", "tensor"), None),
        P(("dp", "tensor")),
        P("dp", None),
        P("pipe", None, "tensor"),
        P("pipe", None, "tensor"),
        P("pipe", "tensor", None),
        P("pipe", None, "tensor"),
        P("pipe", None, "tensor"),
        P("pipe", "tensor", None),
        P("pipe", None),
        P("pipe", None),
    )
    return jax.shard_map(
        shards,
        mesh=mesh,
        in_specs=placed,
        out_specs=P(("dp", "pipe", "tensor"), None),
        check_vma=False,
    )
```

```python
import jax
import jax.numpy as jnp
from jax import lax
from jax.experimental import pallas as pl
from jax.experimental.pallas import tpu as pltpu
from jax.sharding import PartitionSpec as P

HD = 128
CORES = 2
VMEM_LIMIT = 48 * 2**20
UNIT = 128
PLAIN_MOMENTS = 2


def swapped(value):
    pairs = [(source, source ^ 1) for source in range(lax.axis_size("tensor"))]
    return lax.ppermute(value, "tensor", pairs)


def parity():
    return lax.axis_index("tensor") % CORES


def scatter_add(total, left, weight):
    peers = lax.axis_size("tensor")
    chips = peers // CORES
    rows = left.shape[0] // peers
    split = left.reshape(chips, CORES, rows, -1)
    mine = jnp.where(parity() == 0, split[:, 0], split[:, 1])
    other = jnp.where(parity() == 0, split[:, 1], split[:, 0])
    ordered = jnp.concatenate([other, mine], axis=0).reshape(left.shape)
    part = jnp.dot(ordered, weight, preferred_element_type=jnp.float32)
    half = chips * rows
    got = swapped(part[:half].astype(jnp.bfloat16))
    pair = (part[half:] + got.astype(jnp.float32)).astype(jnp.bfloat16)
    blocks = lax.all_to_all(
        pair.reshape(chips, rows, -1),
        "tensor",
        split_axis=0,
        concat_axis=0,
        tiled=True,
        axis_index_groups=[list(range(core, peers, CORES)) for core in range(CORES)],
    )
    for chip in range(chips):
        total = total + blocks[chip].astype(jnp.float32)
    return total


def tables(doc_ids):
    order = jnp.arange(doc_ids.shape[1], dtype=jnp.int32)
    same = doc_ids[:, :, None] == doc_ids[:, None, :]
    seen = jnp.logical_and(same, order[None, :] <= order[:, None])
    places = jnp.sum(seen.astype(jnp.float32), axis=-1) - 1.0
    half = HD // 2
    frequency = 500000.0 ** (-(jnp.arange(half, dtype=jnp.float32) * 2.0 / HD))
    angles = places[:, :, None] * frequency
    cosine, sine = jnp.cos(angles), jnp.sin(angles)
    return jnp.stack(
        [
            jnp.concatenate([cosine, cosine], axis=-1),
            jnp.concatenate([-sine, sine], axis=-1),
            seen.astype(jnp.float32),
        ],
        axis=1,
    )


def normalize(rows_in, gain):
    meansq = jnp.mean(rows_in * rows_in, axis=-1, keepdims=True)
    return (rows_in * lax.rsqrt(meansq + 1e-05) * gain).astype(jnp.bfloat16)


def split_float(values):
    high = values.astype(jnp.bfloat16)
    return high, (values - high.astype(jnp.float32)).astype(jnp.bfloat16)


def attend(queries, keys, values, seen):
    query_high, query_low = split_float(queries)
    key_high, key_low = split_float(keys)
    scores = lax.dot_general(
        jnp.concatenate([query_high, query_high, query_low], axis=1),
        jnp.concatenate([key_high, key_low, key_high], axis=1),
        (((1,), (1,)), ((), ())),
        preferred_element_type=jnp.float32,
    ) * HD ** (-0.5)
    scores = jnp.where(seen > 0.5, scores, jnp.float32(-1e30))
    spread = jnp.exp(scores - jnp.max(scores, axis=-1, keepdims=True))
    weights = (spread / jnp.sum(spread, axis=-1, keepdims=True)).astype(jnp.bfloat16)
    return jnp.dot(weights, values, preferred_element_type=jnp.float32).astype(jnp.bfloat16)


def attend_local(piece, query_local, pair_local, turns):
    cosine, sine, seen = turns

    def turn(head):
        front, back = head[:, : HD // 2], head[:, HD // 2 :]
        return head * cosine + jnp.concatenate([back, front], axis=1) * sine

    queries = turn(jnp.dot(piece, query_local, preferred_element_type=jnp.float32))
    pair = jnp.dot(piece, pair_local, preferred_element_type=jnp.float32)
    mine = jnp.where(parity() == 0, turn(pair), pair)
    partner = swapped(mine.astype(jnp.bfloat16)).astype(mine.dtype)
    keys = jnp.where(parity() == 0, mine, partner)
    values = jnp.where(parity() == 0, partner, mine).astype(jnp.bfloat16)
    return attend(queries, keys, values, seen)


def quarter_weights(query_local, pair_local, out_local):
    chips, parts = lax.axis_size("tensor") // CORES, lax.axis_size("dp")
    turn = lax.axis_index("dp")
    width, columns = query_local.shape
    cut, wide = width // parts, 2 * columns
    rows_in = [
        lax.dynamic_slice_in_dim(local, turn * cut, cut, 0) for local in (query_local, pair_local)
    ]
    columns_out = lax.dynamic_slice_in_dim(out_local, turn * cut, cut, 1)
    blocks = [columns_out[:, at : at + wide] for at in range(0, cut, wide)]
    quarter = jnp.concatenate([jnp.concatenate(rows_in, axis=1)] + blocks, axis=0)
    column = lax.all_gather(quarter, "tensor", axis=0, tiled=True)
    return column.reshape(chips // CORES, CORES, CORES, -1, UNIT, wide)


def whole_weights(column):
    return lax.all_gather(
        lax.dynamic_index_in_dim(column, parity(), 1, keepdims=False), "dp", axis=0
    )


def attention_body(
    x_ref,
    gain_ref,
    turns_ref,
    whole_hbm,
    total_ref,
    normed_ref,
    in_ref,
    out_ref,
    in_sem,
    out_sem,
):
    groups, parts, units, _, columns = in_ref.shape
    tiles, wide = out_ref.shape[1], out_ref.shape[-1]
    rows, width = x_ref.shape
    strip = 16
    fetch_in, fetch_out = [], []
    for group in range(groups):
        for core in range(CORES):
            slot = group * CORES + core
            fetch_in.append(
                pltpu.make_async_copy(
                    whole_hbm.at[:, group, core, pl.ds(0, units)],
                    in_ref.at[group, :, :, :, pl.ds(core * wide, wide)],
                    in_sem.at[slot],
                )
            )
            fetch_out.append(
                pltpu.make_async_copy(
                    whole_hbm.at[:, group, core, pl.ds(units, tiles)],
                    out_ref.at[:, :, slot],
                    out_sem.at[slot],
                )
            )
    for copy in fetch_in + fetch_out:
        copy.start()

    @pl.loop(0, rows // strip)
    def _(index):
        part = pl.ds(pl.multiple_of(index * strip, strip), strip)
        normed_ref[part, :] = normalize(x_ref[part, :].astype(jnp.float32), gain_ref[...])

    cosine, sine, seen = turns_ref[0], turns_ref[1], turns_ref[2]
    seen_twice = jnp.concatenate([seen, seen], axis=0)

    def turn(head):
        return head * cosine + pltpu.roll(head, HD // 2, 1) * sine

    def project(group):
        for core in range(CORES):
            fetch_in[group * CORES + core].wait()
        weight = in_ref[group].reshape(width, columns)
        return jnp.dot(normed_ref[...], weight, preferred_element_type=jnp.float32)

    mixed = []
    heads = project(0)
    for group in range(groups):
        later = project(group + 1) if group + 1 < groups else None
        queries = jnp.concatenate(
            [turn(heads[:, :HD]), turn(heads[:, 2 * HD : 3 * HD])], axis=0
        )
        both = attend(
            queries,
            turn(heads[:, HD : 2 * HD]),
            heads[:, 3 * HD :].astype(jnp.bfloat16),
            seen_twice,
        )
        mixed += [both[:rows], both[rows:]]
        heads = later
    left = jnp.concatenate(mixed, axis=1)
    for copy in fetch_out:
        copy.wait()
    for tile in range(parts * tiles):
        right = out_ref[tile // tiles, tile % tiles].reshape(left.shape[1], wide)
        total_ref[:, tile * wide : (tile + 1) * wide] = jnp.dot(
            left, right, preferred_element_type=jnp.float32
        ).astype(jnp.bfloat16)


def attention_half(everyone, turns, whole, gain):
    rows, width = everyone.shape
    parts, groups, _, units, _, wide = whole.shape
    inner = width // UNIT // parts
    tiles = units - inner
    slots = groups * CORES
    vmem = pl.BlockSpec(memory_space=pltpu.VMEM)
    return pl.pallas_call(
        attention_body,
        in_specs=[vmem] * 3 + [pl.BlockSpec(memory_space=pltpu.HBM)],
        out_specs=vmem,
        scratch_shapes=[
            pltpu.VMEM((rows, width), jnp.bfloat16),
            pltpu.VMEM((groups, parts, inner, UNIT, CORES * wide), jnp.bfloat16),
            pltpu.VMEM((parts, tiles, slots, UNIT, wide), jnp.bfloat16),
            pltpu.SemaphoreType.DMA((slots,)),
            pltpu.SemaphoreType.DMA((slots,)),
        ],
        out_shape=jax.ShapeDtypeStruct((rows, width), jnp.bfloat16),
        compiler_params=pltpu.CompilerParams(vmem_limit_bytes=VMEM_LIMIT),
        cost_estimate=pl.CostEstimate(
            flops=2 * rows * parts * slots * units * UNIT * wide,
            bytes_accessed=2 * parts * slots * units * UNIT * wide,
            transcendentals=2 * rows * rows * groups,
        ),
    )(
        everyone,
        gain[None],
        turns,
        whole,
    )


def run_layer(current, micro_index, turns, layer_weights, whole, column):
    (
        query_local,
        pair_local,
        out_local,
        gate_local,
        up_local,
        down_local,
        gain_attention,
        gain_forward,
    ) = layer_weights
    slab_rows = current.shape[0]
    now = lax.dynamic_index_in_dim(turns, micro_index, 0, keepdims=False)
    everyone = lax.all_gather(current, "tensor", axis=0, tiled=True)
    if whole is not None:
        part = attention_half(everyone, now, whole, gain_attention)
        total = part.astype(jnp.float32) + swapped(part).astype(jnp.float32)
        halfway_all = everyone.astype(jnp.float32) + total
        piece = normalize(halfway_all, gain_forward)
        start = lax.axis_index("tensor") * slab_rows
        halfway = lax.dynamic_slice_in_dim(halfway_all, start, slab_rows, 0)
    else:
        piece = normalize(everyone.astype(jnp.float32), gain_attention)
        mixed = attend_local(piece, query_local, pair_local, now)
        halfway = scatter_add(current.astype(jnp.float32), mixed, out_local)
        if column is not None:
            column, halfway = lax.optimization_barrier((column, halfway))
            whole = whole_weights(column)
        piece = lax.all_gather(normalize(halfway, gain_forward), "tensor", axis=0, tiled=True)
    gate = jnp.dot(piece, gate_local, preferred_element_type=jnp.float32)
    upward = jnp.dot(piece, up_local, preferred_element_type=jnp.float32)
    hidden = (jax.nn.silu(gate) * upward).astype(jnp.bfloat16)
    result = scatter_add(halfway, hidden, down_local)
    return result if column is None else (result, whole)


def pass_on(result, moment, micro_count):
    last = lax.axis_size("pipe") - 1
    pairs = [(i, i + 1) for i in range(last) if 0 <= moment - i < micro_count]
    if moment >= last:
        pairs.append((last, moment - last))
    return lax.ppermute(result.astype(jnp.bfloat16), "pipe", pairs)


def regroup(tokens, destination, group_count, group_span, micro_rows, slab_rows):
    held_rows, width = tokens.shape
    capacity = held_rows // 2
    slots = group_count * capacity
    target = destination // group_span
    within = destination % group_span
    landing = within // micro_rows * slab_rows + within % slab_rows
    order = jnp.arange(held_rows, dtype=jnp.int32)
    ahead = jnp.logical_and(target[:, None] == target[None, :], order[None, :] < order[:, None])
    slot_index = target * capacity + jnp.sum(ahead.astype(jnp.int32), axis=1)
    to_slot = jnp.arange(slots, dtype=jnp.int32)[:, None] == slot_index[None, :]
    mark = jnp.broadcast_to((landing + 1).astype(jnp.bfloat16)[:, None], (held_rows, HD))
    sent = jnp.dot(
        to_slot.astype(jnp.bfloat16),
        jnp.concatenate([tokens, mark], axis=1),
        preferred_element_type=jnp.float32,
    ).astype(jnp.bfloat16)
    got = lax.all_to_all(
        sent.reshape(group_count, capacity, width + HD),
        "dp",
        split_axis=0,
        concat_axis=0,
        tiled=True,
    ).reshape(slots, width + HD)
    place = got[:, width].astype(jnp.int32) - 1
    to_row = order[:, None] == place[None, :]
    return jnp.dot(
        to_row.astype(jnp.bfloat16), got[:, :width], preferred_element_type=jnp.float32
    ).astype(jnp.bfloat16)


def shards(
    tokens,
    destination,
    segments,
    query_weight,
    key_value_weight,
    out_weight,
    gate_weight,
    up_weight,
    down_weight,
    attention_gain,
    forward_gain,
):
    pipe_count = lax.axis_size("pipe")
    micro_count, micro_rows = segments.shape
    slab_rows = micro_rows // lax.axis_size("tensor")
    width = tokens.shape[1]
    column = quarter_weights(query_weight[0], key_value_weight[0], out_weight[0])
    whole = None
    regrouped = regroup(
        tokens,
        destination,
        lax.axis_size("dp"),
        micro_count * micro_rows,
        micro_rows,
        slab_rows,
    )
    micro_batches = regrouped.reshape(micro_count, slab_rows, width)
    turns = tables(segments)
    layer_weights = (
        query_weight[0],
        key_value_weight[0],
        out_weight[0],
        gate_weight[0],
        up_weight[0],
        down_weight[0],
        attention_gain[0],
        forward_gain[0],
    )
    phase_index = lax.axis_index("pipe")
    carried = jnp.zeros((slab_rows, width), jnp.bfloat16)
    out = jnp.zeros((slab_rows, width), jnp.float32)
    for moment in range(micro_count + pipe_count - 1):
        current = carried
        if moment < micro_count:
            current = jnp.where(phase_index == 0, micro_batches[moment], carried)
        micro_index = jnp.clip(moment - phase_index, 0, micro_count - 1)
        result = run_layer(
            current,
            micro_index,
            turns,
            layer_weights,
            None if moment < PLAIN_MOMENTS else whole,
            column if moment == 0 else None,
        )
        if moment == 0:
            result, whole = result
        home = moment - (pipe_count - 1)
        if moment < micro_count + pipe_count - 2:
            carried = pass_on(result, moment, micro_count)
            if home >= 0:
                out = jnp.where(phase_index == home, carried.astype(jnp.float32), out)
        else:
            out = jnp.where(phase_index == home, result, out)
    return out


def solution(mesh):
    placed = (
        P(("dp", "tensor"), None),
        P(("dp", "tensor")),
        P("dp", None),
        P("pipe", None, "tensor"),
        P("pipe", None, "tensor"),
        P("pipe", "tensor", None),
        P("pipe", None, "tensor"),
        P("pipe", None, "tensor"),
        P("pipe", "tensor", None),
        P("pipe", None),
        P("pipe", None),
    )
    return jax.shard_map(
        shards,
        mesh=mesh,
        in_specs=placed,
        out_specs=P(("dp", "pipe", "tensor"), None),
        check_vma=False,
    )
```

```python
import jax
import jax.numpy as jnp
from jax import lax
from jax.experimental import pallas as pl
from jax.experimental.pallas import tpu as pltpu
from jax.sharding import PartitionSpec as P

HD = 128
CORES = 2
VMEM_LIMIT = 28 * 2**20
UNIT = 128
PLAIN_MOMENTS = 1


def swapped(value):
    pairs = [(source, source ^ 1) for source in range(lax.axis_size("tensor"))]
    return lax.ppermute(value, "tensor", pairs)


def parity():
    return lax.axis_index("tensor") % CORES


def scatter_add(total, left, weight):
    peers = lax.axis_size("tensor")
    chips = peers // CORES
    rows = left.shape[0] // peers
    split = left.reshape(chips, CORES, rows, -1)
    mine = jnp.where(parity() == 0, split[:, 0], split[:, 1])
    other = jnp.where(parity() == 0, split[:, 1], split[:, 0])
    ordered = jnp.concatenate([other, mine], axis=0).reshape(left.shape)
    part = jnp.dot(ordered, weight, preferred_element_type=jnp.float32)
    half = chips * rows
    got = swapped(part[:half].astype(jnp.bfloat16))
    pair = (part[half:] + got.astype(jnp.float32)).astype(jnp.bfloat16)
    blocks = lax.all_to_all(
        pair.reshape(chips, rows, -1),
        "tensor",
        split_axis=0,
        concat_axis=0,
        tiled=True,
        axis_index_groups=[list(range(core, peers, CORES)) for core in range(CORES)],
    )
    for chip in range(chips):
        total = total + blocks[chip].astype(jnp.float32)
    return total


def tables(doc_ids):
    order = jnp.arange(doc_ids.shape[1], dtype=jnp.int32)
    same = doc_ids[:, :, None] == doc_ids[:, None, :]
    seen = jnp.logical_and(same, order[None, :] <= order[:, None])
    places = jnp.sum(seen.astype(jnp.float32), axis=-1) - 1.0
    half = HD // 2
    frequency = 500000.0 ** (-(jnp.arange(half, dtype=jnp.float32) * 2.0 / HD))
    angles = places[:, :, None] * frequency
    cosine, sine = jnp.cos(angles), jnp.sin(angles)
    return jnp.stack(
        [
            jnp.concatenate([cosine, cosine], axis=-1),
            jnp.concatenate([-sine, sine], axis=-1),
            seen.astype(jnp.float32),
        ],
        axis=1,
    )


def normalize(rows_in, gain):
    meansq = jnp.mean(rows_in * rows_in, axis=-1, keepdims=True)
    return (rows_in * lax.rsqrt(meansq + 1e-05) * gain).astype(jnp.bfloat16)


def split_float(values):
    high = values.astype(jnp.bfloat16)
    return high, (values - high.astype(jnp.float32)).astype(jnp.bfloat16)


def attend(queries, keys, values, seen):
    query_high, query_low = split_float(queries)
    key_high, key_low = split_float(keys)
    scores = lax.dot_general(
        jnp.concatenate([query_high, query_high, query_low], axis=1),
        jnp.concatenate([key_high, key_low, key_high], axis=1),
        (((1,), (1,)), ((), ())),
        preferred_element_type=jnp.float32,
    ) * HD ** (-0.5)
    scores = jnp.where(seen > 0.5, scores, jnp.float32(-1e30))
    spread = jnp.exp(scores - jnp.max(scores, axis=-1, keepdims=True))
    weights = (spread / jnp.sum(spread, axis=-1, keepdims=True)).astype(jnp.bfloat16)
    return jnp.dot(weights, values, preferred_element_type=jnp.float32).astype(jnp.bfloat16)


def attend_local(piece, query_local, pair_local, turns):
    cosine, sine, seen = turns

    def turn(head):
        front, back = head[:, : HD // 2], head[:, HD // 2 :]
        return head * cosine + jnp.concatenate([back, front], axis=1) * sine

    queries = turn(jnp.dot(piece, query_local, preferred_element_type=jnp.float32))
    pair = jnp.dot(piece, pair_local, preferred_element_type=jnp.float32)
    mine = jnp.where(parity() == 0, turn(pair), pair)
    partner = swapped(mine.astype(jnp.bfloat16)).astype(mine.dtype)
    keys = jnp.where(parity() == 0, mine, partner)
    values = jnp.where(parity() == 0, partner, mine).astype(jnp.bfloat16)
    return attend(queries, keys, values, seen)


def whole_weights(query_local, pair_local, out_local):
    chips, parts = lax.axis_size("tensor") // CORES, lax.axis_size("dp")
    turn = lax.axis_index("dp")
    width, columns = query_local.shape
    cut, wide = width // parts, 2 * columns
    rows_in = [
        lax.dynamic_slice_in_dim(local, turn * cut, cut, 0) for local in (query_local, pair_local)
    ]
    columns_out = lax.dynamic_slice_in_dim(out_local, turn * cut, cut, 1)
    blocks = [columns_out[:, at : at + wide] for at in range(0, cut, wide)]
    quarter = jnp.concatenate([jnp.concatenate(rows_in, axis=1)] + blocks, axis=0)
    whole = lax.all_gather(quarter, ("dp", "tensor"), axis=0, tiled=True)
    return whole.reshape(parts, chips // CORES, CORES, CORES, -1, UNIT, wide)


def attention_body(
    where_ref,
    x_ref,
    gain_ref,
    turns_ref,
    whole_hbm,
    total_ref,
    normed_ref,
    in_ref,
    out_ref,
    in_sem,
    out_sem,
):
    groups, parts, units, _, columns = in_ref.shape
    tiles, wide = out_ref.shape[1], out_ref.shape[-1]
    rows, width = x_ref.shape
    strip = 16
    half = where_ref[0]
    fetch_in, fetch_out = [], []
    for group in range(groups):
        for core in range(CORES):
            slot = group * CORES + core
            fetch_in.append(
                pltpu.make_async_copy(
                    whole_hbm.at[:, group, half, core, pl.ds(0, units)],
                    in_ref.at[group, :, :, :, pl.ds(core * wide, wide)],
                    in_sem.at[slot],
                )
            )
            fetch_out.append(
                pltpu.make_async_copy(
                    whole_hbm.at[:, group, half, core, pl.ds(units, tiles)],
                    out_ref.at[:, :, slot],
                    out_sem.at[slot],
                )
            )
    for copy in fetch_in + fetch_out:
        copy.start()

    @pl.loop(0, rows // strip)
    def _(index):
        part = pl.ds(pl.multiple_of(index * strip, strip), strip)
        normed_ref[part, :] = normalize(x_ref[part, :].astype(jnp.float32), gain_ref[...])

    cosine, sine, seen = turns_ref[0], turns_ref[1], turns_ref[2]
    seen_twice = jnp.concatenate([seen, seen], axis=0)

    def turn(head):
        return head * cosine + pltpu.roll(head, HD // 2, 1) * sine

    def project(group):
        for core in range(CORES):
            fetch_in[group * CORES + core].wait()
        weight = in_ref[group].reshape(width, columns)
        return jnp.dot(normed_ref[...], weight, preferred_element_type=jnp.float32)

    mixed = []
    heads = project(0)
    for group in range(groups):
        later = project(group + 1) if group + 1 < groups else None
        queries = jnp.concatenate(
            [turn(heads[:, :HD]), turn(heads[:, 2 * HD : 3 * HD])], axis=0
        )
        both = attend(
            queries,
            turn(heads[:, HD : 2 * HD]),
            heads[:, 3 * HD :].astype(jnp.bfloat16),
            seen_twice,
        )
        mixed += [both[:rows], both[rows:]]
        heads = later
    left = jnp.concatenate(mixed, axis=1)
    for copy in fetch_out:
        copy.wait()
    for tile in range(parts * tiles):
        right = out_ref[tile // tiles, tile % tiles].reshape(left.shape[1], wide)
        total_ref[:, tile * wide : (tile + 1) * wide] = jnp.dot(
            left, right, preferred_element_type=jnp.float32
        ).astype(jnp.bfloat16)


def attention_half(everyone, turns, whole, gain):
    rows, width = everyone.shape
    parts, groups, _, _, units, _, wide = whole.shape
    inner = width // UNIT // parts
    tiles = units - inner
    slots = groups * CORES
    vmem = pl.BlockSpec(memory_space=pltpu.VMEM)
    return pl.pallas_call(
        attention_body,
        in_specs=[pl.BlockSpec(memory_space=pltpu.SMEM)]
        + [vmem] * 3
        + [pl.BlockSpec(memory_space=pltpu.HBM)],
        out_specs=vmem,
        scratch_shapes=[
            pltpu.VMEM((rows, width), jnp.bfloat16),
            pltpu.VMEM((groups, parts, inner, UNIT, CORES * wide), jnp.bfloat16),
            pltpu.VMEM((parts, tiles, slots, UNIT, wide), jnp.bfloat16),
            pltpu.SemaphoreType.DMA((slots,)),
            pltpu.SemaphoreType.DMA((slots,)),
        ],
        out_shape=jax.ShapeDtypeStruct((rows, width), jnp.bfloat16),
        compiler_params=pltpu.CompilerParams(vmem_limit_bytes=VMEM_LIMIT),
        cost_estimate=pl.CostEstimate(
            flops=2 * rows * parts * slots * units * UNIT * wide,
            bytes_accessed=2 * parts * slots * units * UNIT * wide,
            transcendentals=2 * rows * rows * groups,
        ),
    )(
        parity().astype(jnp.int32)[None],
        everyone,
        gain[None],
        turns,
        whole,
    )


def run_layer(current, micro_index, turns, layer_weights, whole):
    (
        query_local,
        pair_local,
        out_local,
        gate_local,
        up_local,
        down_local,
        gain_attention,
        gain_forward,
    ) = layer_weights
    slab_rows = current.shape[0]
    now = lax.dynamic_index_in_dim(turns, micro_index, 0, keepdims=False)
    everyone = lax.all_gather(current, "tensor", axis=0, tiled=True)
    if whole is not None:
        part = attention_half(everyone, now, whole, gain_attention)
        total = part.astype(jnp.float32) + swapped(part).astype(jnp.float32)
        halfway_all = everyone.astype(jnp.float32) + total
        piece = normalize(halfway_all, gain_forward)
        start = lax.axis_index("tensor") * slab_rows
        halfway = lax.dynamic_slice_in_dim(halfway_all, start, slab_rows, 0)
    else:
        piece = normalize(everyone.astype(jnp.float32), gain_attention)
        mixed = attend_local(piece, query_local, pair_local, now)
        halfway = scatter_add(current.astype(jnp.float32), mixed, out_local)
        piece = lax.all_gather(normalize(halfway, gain_forward), "tensor", axis=0, tiled=True)
    gate = jnp.dot(piece, gate_local, preferred_element_type=jnp.float32)
    upward = jnp.dot(piece, up_local, preferred_element_type=jnp.float32)
    hidden = (jax.nn.silu(gate) * upward).astype(jnp.bfloat16)
    return scatter_add(halfway, hidden, down_local)


def pass_on(result, moment, micro_count):
    last = lax.axis_size("pipe") - 1
    pairs = [(i, i + 1) for i in range(last) if 0 <= moment - i < micro_count]
    if moment >= last:
        pairs.append((last, moment - last))
    return lax.ppermute(result.astype(jnp.bfloat16), "pipe", pairs)


def regroup(tokens, destination, group_count, group_span, micro_rows, slab_rows):
    held_rows, width = tokens.shape
    capacity = held_rows // 2
    slots = group_count * capacity
    target = destination // group_span
    within = destination % group_span
    landing = within // micro_rows * slab_rows + within % slab_rows
    order = jnp.arange(held_rows, dtype=jnp.int32)
    ahead = jnp.logical_and(target[:, None] == target[None, :], order[None, :] < order[:, None])
    slot_index = target * capacity + jnp.sum(ahead.astype(jnp.int32), axis=1)
    to_slot = jnp.arange(slots, dtype=jnp.int32)[:, None] == slot_index[None, :]
    mark = jnp.broadcast_to((landing + 1).astype(jnp.bfloat16)[:, None], (held_rows, HD))
    sent = jnp.dot(
        to_slot.astype(jnp.bfloat16),
        jnp.concatenate([tokens, mark], axis=1),
        preferred_element_type=jnp.float32,
    ).astype(jnp.bfloat16)
    got = lax.all_to_all(
        sent.reshape(group_count, capacity, width + HD),
        "dp",
        split_axis=0,
        concat_axis=0,
        tiled=True,
    ).reshape(slots, width + HD)
    place = got[:, width].astype(jnp.int32) - 1
    to_row = order[:, None] == place[None, :]
    return jnp.dot(
        to_row.astype(jnp.bfloat16), got[:, :width], preferred_element_type=jnp.float32
    ).astype(jnp.bfloat16)


def shards(
    tokens,
    destination,
    segments,
    query_weight,
    key_value_weight,
    out_weight,
    gate_weight,
    up_weight,
    down_weight,
    attention_gain,
    forward_gain,
):
    pipe_count = lax.axis_size("pipe")
    micro_count, micro_rows = segments.shape
    slab_rows = micro_rows // lax.axis_size("tensor")
    width = tokens.shape[1]
    whole = whole_weights(query_weight[0], key_value_weight[0], out_weight[0])
    regrouped = regroup(
        tokens,
        destination,
        lax.axis_size("dp"),
        micro_count * micro_rows,
        micro_rows,
        slab_rows,
    )
    micro_batches = regrouped.reshape(micro_count, slab_rows, width)
    turns = tables(segments)
    layer_weights = (
        query_weight[0],
        key_value_weight[0],
        out_weight[0],
        gate_weight[0],
        up_weight[0],
        down_weight[0],
        attention_gain[0],
        forward_gain[0],
    )
    phase_index = lax.axis_index("pipe")
    carried = jnp.zeros((slab_rows, width), jnp.bfloat16)
    out = jnp.zeros((slab_rows, width), jnp.float32)
    for moment in range(micro_count + pipe_count - 1):
        current = carried
        if moment < micro_count:
            current = jnp.where(phase_index == 0, micro_batches[moment], carried)
        micro_index = jnp.clip(moment - phase_index, 0, micro_count - 1)
        result = run_layer(
            current,
            micro_index,
            turns,
            layer_weights,
            None if moment < PLAIN_MOMENTS else whole,
        )
        home = moment - (pipe_count - 1)
        if moment < micro_count + pipe_count - 2:
            carried = pass_on(result, moment, micro_count)
            if home >= 0:
                out = jnp.where(phase_index == home, carried.astype(jnp.float32), out)
        else:
            out = jnp.where(phase_index == home, result, out)
    return out


def solution(mesh):
    placed = (
        P(("dp", "tensor"), None),
        P(("dp", "tensor")),
        P("dp", None),
        P("pipe", None, "tensor"),
        P("pipe", None, "tensor"),
        P("pipe", "tensor", None),
        P("pipe", None, "tensor"),
        P("pipe", None, "tensor"),
        P("pipe", "tensor", None),
        P("pipe", None),
        P("pipe", None),
    )
    return jax.shard_map(
        shards,
        mesh=mesh,
        in_specs=placed,
        out_specs=P(("dp", "pipe", "tensor"), None),
        check_vma=False,
    )
```

```python
import jax
import jax.numpy as jnp
from jax import lax
from jax.experimental import pallas as pl
from jax.experimental.pallas import tpu as pltpu
from jax.sharding import PartitionSpec as P

HD = 128
CORES = 2
VMEM_LIMIT = 28 * 2**20
UNIT = 128
PLAIN_MOMENTS = 1


def swapped(value):
    pairs = [(source, source ^ 1) for source in range(lax.axis_size("tensor"))]
    return lax.ppermute(value, "tensor", pairs)


def parity():
    return lax.axis_index("tensor") % CORES


def scatter_add(total, left, weight):
    peers = lax.axis_size("tensor")
    chips = peers // CORES
    rows = left.shape[0] // peers
    split = left.reshape(chips, CORES, rows, -1)
    mine = jnp.where(parity() == 0, split[:, 0], split[:, 1])
    other = jnp.where(parity() == 0, split[:, 1], split[:, 0])
    ordered = jnp.concatenate([other, mine], axis=0).reshape(left.shape)
    part = jnp.dot(ordered, weight, preferred_element_type=jnp.float32)
    half = chips * rows
    got = swapped(part[:half].astype(jnp.bfloat16))
    pair = (part[half:] + got.astype(jnp.float32)).astype(jnp.bfloat16)
    blocks = lax.all_to_all(
        pair.reshape(chips, rows, -1),
        "tensor",
        split_axis=0,
        concat_axis=0,
        tiled=True,
        axis_index_groups=[list(range(core, peers, CORES)) for core in range(CORES)],
    )
    for chip in range(chips):
        total = total + blocks[chip].astype(jnp.float32)
    return total


def tables(doc_ids):
    order = jnp.arange(doc_ids.shape[1], dtype=jnp.int32)
    same = doc_ids[:, :, None] == doc_ids[:, None, :]
    seen = jnp.logical_and(same, order[None, :] <= order[:, None])
    places = jnp.sum(seen.astype(jnp.float32), axis=-1) - 1.0
    half = HD // 2
    frequency = 500000.0 ** (-(jnp.arange(half, dtype=jnp.float32) * 2.0 / HD))
    angles = places[:, :, None] * frequency
    cosine, sine = jnp.cos(angles), jnp.sin(angles)
    return jnp.stack(
        [
            jnp.concatenate([cosine, cosine], axis=-1),
            jnp.concatenate([-sine, sine], axis=-1),
            seen.astype(jnp.float32),
        ],
        axis=1,
    )


def normalize(rows_in, gain):
    meansq = jnp.mean(rows_in * rows_in, axis=-1, keepdims=True)
    return (rows_in * lax.rsqrt(meansq + 1e-05) * gain).astype(jnp.bfloat16)


def split_float(values):
    high = values.astype(jnp.bfloat16)
    return high, (values - high.astype(jnp.float32)).astype(jnp.bfloat16)


def attend(queries, keys, values, seen):
    query_high, query_low = split_float(queries)
    key_high, key_low = split_float(keys)
    scores = lax.dot_general(
        jnp.concatenate([query_high, query_high, query_low], axis=1),
        jnp.concatenate([key_high, key_low, key_high], axis=1),
        (((1,), (1,)), ((), ())),
        preferred_element_type=jnp.float32,
    ) * HD ** (-0.5)
    scores = jnp.where(seen > 0.5, scores, jnp.float32(-1e30))
    spread = jnp.exp(scores - jnp.max(scores, axis=-1, keepdims=True))
    weights = (spread / jnp.sum(spread, axis=-1, keepdims=True)).astype(jnp.bfloat16)
    return jnp.dot(weights, values, preferred_element_type=jnp.float32).astype(jnp.bfloat16)


def attend_local(piece, query_local, pair_local, turns):
    cosine, sine, seen = turns

    def turn(head):
        front, back = head[:, : HD // 2], head[:, HD // 2 :]
        return head * cosine + jnp.concatenate([back, front], axis=1) * sine

    queries = turn(jnp.dot(piece, query_local, preferred_element_type=jnp.float32))
    pair = jnp.dot(piece, pair_local, preferred_element_type=jnp.float32)
    mine = jnp.where(parity() == 0, turn(pair), pair)
    partner = swapped(mine.astype(jnp.bfloat16)).astype(mine.dtype)
    keys = jnp.where(parity() == 0, mine, partner)
    values = jnp.where(parity() == 0, partner, mine).astype(jnp.bfloat16)
    return attend(queries, keys, values, seen)


def whole_weights(query_local, pair_local, out_local):
    chips, parts = lax.axis_size("tensor") // CORES, lax.axis_size("dp")
    turn = lax.axis_index("dp")
    width, columns = query_local.shape
    cut, wide = width // parts, 2 * columns
    rows_in = [
        lax.dynamic_slice_in_dim(local, turn * cut, cut, 0) for local in (query_local, pair_local)
    ]
    columns_out = lax.dynamic_slice_in_dim(out_local, turn * cut, cut, 1)
    blocks = [columns_out[:, at : at + wide] for at in range(0, cut, wide)]
    quarter = jnp.concatenate([jnp.concatenate(rows_in, axis=1)] + blocks, axis=0)
    whole = lax.all_gather(quarter, ("dp", "tensor"), axis=0, tiled=True)
    return whole.reshape(parts, chips // CORES, CORES, CORES, -1, UNIT, wide)


def attention_body(
    where_ref,
    x_ref,
    gain_ref,
    turns_ref,
    whole_hbm,
    total_ref,
    normed_ref,
    in_ref,
    out_ref,
    in_sem,
    out_sem,
):
    groups, parts, units, _, columns = in_ref.shape
    tiles, wide = out_ref.shape[1], out_ref.shape[-1]
    rows, width = x_ref.shape
    strip = 16
    half = where_ref[0]
    fetch_in, fetch_out = [], []
    for group in range(groups):
        for core in range(CORES):
            slot = group * CORES + core
            fetch_in.append(
                pltpu.make_async_copy(
                    whole_hbm.at[:, group, half, core, pl.ds(0, units)],
                    in_ref.at[group, :, :, :, pl.ds(core * wide, wide)],
                    in_sem.at[slot],
                )
            )
            fetch_out.append(
                pltpu.make_async_copy(
                    whole_hbm.at[:, group, half, core, pl.ds(units, tiles)],
                    out_ref.at[:, :, slot],
                    out_sem.at[slot],
                )
            )
    for copy in fetch_in + fetch_out:
        copy.start()

    @pl.loop(0, rows // strip)
    def _(index):
        part = pl.ds(pl.multiple_of(index * strip, strip), strip)
        normed_ref[part, :] = normalize(x_ref[part, :].astype(jnp.float32), gain_ref[...])

    cosine, sine, seen = turns_ref[0], turns_ref[1], turns_ref[2]
    seen_twice = jnp.concatenate([seen, seen], axis=0)

    def turn(head):
        return head * cosine + pltpu.roll(head, HD // 2, 1) * sine

    def project(group):
        for core in range(CORES):
            fetch_in[group * CORES + core].wait()
        weight = in_ref[group].reshape(width, columns)
        return jnp.dot(normed_ref[...], weight, preferred_element_type=jnp.float32)

    mixed = []
    heads = project(0)
    for group in range(groups):
        later = project(group + 1) if group + 1 < groups else None
        queries = jnp.concatenate(
            [turn(heads[:, :HD]), turn(heads[:, 2 * HD : 3 * HD])], axis=0
        )
        both = attend(
            queries,
            turn(heads[:, HD : 2 * HD]),
            heads[:, 3 * HD :].astype(jnp.bfloat16),
            seen_twice,
        )
        mixed += [both[:rows], both[rows:]]
        heads = later
    left = jnp.concatenate(mixed, axis=1)
    for copy in fetch_out:
        copy.wait()
    for tile in range(parts * tiles):
        right = out_ref[tile // tiles, tile % tiles].reshape(left.shape[1], wide)
        total_ref[:, tile * wide : (tile + 1) * wide] = jnp.dot(
            left, right, preferred_element_type=jnp.float32
        ).astype(jnp.bfloat16)


def attention_half(everyone, turns, whole, gain):
    rows, width = everyone.shape
    parts, groups, _, _, units, _, wide = whole.shape
    inner = width // UNIT // parts
    tiles = units - inner
    slots = groups * CORES
    vmem = pl.BlockSpec(memory_space=pltpu.VMEM)
    return pl.pallas_call(
        attention_body,
        in_specs=[pl.BlockSpec(memory_space=pltpu.SMEM)]
        + [vmem] * 3
        + [pl.BlockSpec(memory_space=pltpu.HBM)],
        out_specs=vmem,
        scratch_shapes=[
            pltpu.VMEM((rows, width), jnp.bfloat16),
            pltpu.VMEM((groups, parts, inner, UNIT, CORES * wide), jnp.bfloat16),
            pltpu.VMEM((parts, tiles, slots, UNIT, wide), jnp.bfloat16),
            pltpu.SemaphoreType.DMA((slots,)),
            pltpu.SemaphoreType.DMA((slots,)),
        ],
        out_shape=jax.ShapeDtypeStruct((rows, width), jnp.bfloat16),
        compiler_params=pltpu.CompilerParams(vmem_limit_bytes=VMEM_LIMIT),
        cost_estimate=pl.CostEstimate(
            flops=2 * rows * parts * slots * units * UNIT * wide,
            bytes_accessed=2 * parts * slots * units * UNIT * wide,
            transcendentals=2 * rows * rows * groups,
        ),
    )(
        parity().astype(jnp.int32)[None],
        everyone,
        gain[None],
        turns,
        whole,
    )


def run_layer(current, micro_index, turns, layer_weights, whole):
    (
        query_local,
        pair_local,
        out_local,
        gate_local,
        up_local,
        down_local,
        gain_attention,
        gain_forward,
    ) = layer_weights
    slab_rows = current.shape[0]
    now = lax.dynamic_index_in_dim(turns, micro_index, 0, keepdims=False)
    everyone = lax.all_gather(current, "tensor", axis=0, tiled=True)
    if whole is not None:
        part = attention_half(everyone, now, whole, gain_attention)
        total = part.astype(jnp.float32) + swapped(part).astype(jnp.float32)
        halfway_all = everyone.astype(jnp.float32) + total
        piece = normalize(halfway_all, gain_forward)
        start = lax.axis_index("tensor") * slab_rows
        halfway = lax.dynamic_slice_in_dim(halfway_all, start, slab_rows, 0)
    else:
        piece = normalize(everyone.astype(jnp.float32), gain_attention)
        mixed = attend_local(piece, query_local, pair_local, now)
        halfway = scatter_add(current.astype(jnp.float32), mixed, out_local)
        piece = lax.all_gather(normalize(halfway, gain_forward), "tensor", axis=0, tiled=True)
    gate = jnp.dot(piece, gate_local, preferred_element_type=jnp.float32)
    upward = jnp.dot(piece, up_local, preferred_element_type=jnp.float32)
    hidden = (jax.nn.silu(gate) * upward).astype(jnp.bfloat16)
    return scatter_add(halfway, hidden, down_local)


def pass_on(result, moment, micro_batches):
    last = lax.axis_size("pipe") - 1
    micro_count = micro_batches.shape[0]
    pairs = [(i, i + 1) for i in range(last) if 0 <= moment - i < micro_count]
    sent = result.astype(jnp.bfloat16)
    if moment >= last:
        pairs.append((last, moment - last))
    elif moment + 1 < micro_count:
        pairs.append((last, 0))
        sent = jnp.where(lax.axis_index("pipe") == last, micro_batches[moment + 1], sent)
    return lax.ppermute(sent, "pipe", pairs)


def regroup(tokens, destination, group_count, group_span, micro_rows, slab_rows):
    held_rows, width = tokens.shape
    capacity = held_rows // 2
    slots = group_count * capacity
    target = destination // group_span
    within = destination % group_span
    landing = within // micro_rows * slab_rows + within % slab_rows
    order = jnp.arange(held_rows, dtype=jnp.int32)
    ahead = jnp.logical_and(target[:, None] == target[None, :], order[None, :] < order[:, None])
    slot_index = target * capacity + jnp.sum(ahead.astype(jnp.int32), axis=1)
    to_slot = jnp.arange(slots, dtype=jnp.int32)[:, None] == slot_index[None, :]
    mark = jnp.broadcast_to((landing + 1).astype(jnp.bfloat16)[:, None], (held_rows, HD))
    sent = jnp.dot(
        to_slot.astype(jnp.bfloat16),
        jnp.concatenate([tokens, mark], axis=1),
        preferred_element_type=jnp.float32,
    ).astype(jnp.bfloat16)
    got = lax.all_to_all(
        sent.reshape(group_count, capacity, width + HD),
        "dp",
        split_axis=0,
        concat_axis=0,
        tiled=True,
    ).reshape(slots, width + HD)
    place = got[:, width].astype(jnp.int32) - 1
    to_row = order[:, None] == place[None, :]
    return jnp.dot(
        to_row.astype(jnp.bfloat16), got[:, :width], preferred_element_type=jnp.float32
    ).astype(jnp.bfloat16)


def shards(
    tokens,
    destination,
    segments,
    query_weight,
    key_value_weight,
    out_weight,
    gate_weight,
    up_weight,
    down_weight,
    attention_gain,
    forward_gain,
):
    pipe_count = lax.axis_size("pipe")
    micro_count, micro_rows = segments.shape
    slab_rows = micro_rows // lax.axis_size("tensor")
    width = tokens.shape[1]
    whole = whole_weights(query_weight[0], key_value_weight[0], out_weight[0])
    regrouped = regroup(
        tokens,
        destination,
        lax.axis_size("dp"),
        micro_count * micro_rows,
        micro_rows,
        slab_rows,
    )
    micro_batches = regrouped.reshape(micro_count, slab_rows, width)
    turns = tables(segments)
    layer_weights = (
        query_weight[0],
        key_value_weight[0],
        out_weight[0],
        gate_weight[0],
        up_weight[0],
        down_weight[0],
        attention_gain[0],
        forward_gain[0],
    )
    phase_index = lax.axis_index("pipe")
    carried = micro_batches[0]
    out = jnp.zeros((slab_rows, width), jnp.float32)
    for moment in range(micro_count + pipe_count - 1):
        current = carried
        if pipe_count <= moment < micro_count:
            current = jnp.where(phase_index == 0, micro_batches[moment], carried)
        micro_index = jnp.clip(moment - phase_index, 0, micro_count - 1)
        result = run_layer(
            current,
            micro_index,
            turns,
            layer_weights,
            None if moment < PLAIN_MOMENTS else whole,
        )
        home = moment - (pipe_count - 1)
        if moment < micro_count + pipe_count - 2:
            carried = pass_on(result, moment, micro_batches)
            if home >= 0:
                out = jnp.where(phase_index == home, carried.astype(jnp.float32), out)
        else:
            out = jnp.where(phase_index == home, result, out)
    return out


def solution(mesh):
    placed = (
        P(("dp", "tensor"), None),
        P(("dp", "tensor")),
        P("dp", None),
        P("pipe", None, "tensor"),
        P("pipe", None, "tensor"),
        P("pipe", "tensor", None),
        P("pipe", None, "tensor"),
        P("pipe", None, "tensor"),
        P("pipe", "tensor", None),
        P("pipe", None),
        P("pipe", None),
    )
    return jax.shard_map(
        shards,
        mesh=mesh,
        in_specs=placed,
        out_specs=P(("dp", "pipe", "tensor"), None),
        check_vma=False,
    )
```
